32 devices in a mesh: tensor: 4 (over z), expert: 8 (over y, x, core).
Axes of the slice: x: 2, y: 2, z: 4, core: 2. Of those that a mesh axis runs over, the one named last changes fastest.
Arguments:
- queries: bfloat16 [512, 64, 576], P('expert', 'tensor'), may hold values from -50 to 50
- latent_cache: bfloat16 [8192, 576], P('expert'), may hold values from -5 to 5
- new_latents: bfloat16 [512, 576], P('expert'), may hold values from -5 to 5
- residual: bfloat16 [512, 3584], P(('expert', 'tensor')), may hold values from -6 to 6
- w_uv: bfloat16 [32768, 128], P(('tensor', 'expert')), may hold values from -0.25 to 0.25
- w_out: bfloat16 [8192, 3584], P(('tensor', 'expert')), may hold values from -0.0625 to 0.0625
- norm_gain: float32 [3584], replicated, may hold values from 0.25 to 1.75
- expert_ids: int32 [512, 8], P('expert'), may hold values from 0 to 31, all different within a row; in each aligned block of 64 rows (0 to 63, 64 to 127, ...) at most 32 rows name the same one
- gate_weights: float32 [512, 8], P('expert'), may hold values from 0.1 to 0.6
- w_gate: bfloat16 [32, 3584, 1024], P('expert', None, 'tensor'), may hold values from -0.09375 to 0.09375
- w_up: bfloat16 [32, 3584, 1024], P('expert', None, 'tensor'), may hold values from -0.09375 to 0.09375
- w_down: bfloat16 [32, 1024, 3584], P('expert', 'tensor'), may hold values from -0.1875 to 0.1875
Outputs:
- layer_out: bfloat16 [512, 3584], P(('expert', 'tensor'))
The draws below stay inside these ranges and needn't reach their ends.
Inputs may be any that keep to these rules, and one draw needn't show every extreme that they name: `expert_ids`: within each token group of 64 tokens no expert is chosen by more than 32 routes, some expert by exactly 32; a token names 8 different experts.
All inputs are finite; a program needn't handle non-finite values.
Results may differ from the reference program's by a relative error of at most 0.01.
Values may be sent and summed in bfloat16 or wider, within the bound.
A program may use at most 128 MiB of HBM per device.

```python
import math
import jax
import jax.numpy as jnp
import numpy as np
from jax import lax

D = 3584
HEADS = 64
LATENT = 512
ROPE = 64
VDIM = 128
QDIM = 576
FF = 1024
EXPERTS = 32
TOP = 8
TOK_GRP = 64
CTX = 1024
CAP = 32
TOKENS = 512
N_TENSOR = 4
N_EXPERT = 8


def draw_latent_cache(key, part):
    values_all = jnp.clip(jax.random.normal(jax.random.fold_in(key, 3), (N_EXPERT, CTX, QDIM), jnp.float32), -5.0, 5.0)
    return values_all.reshape(N_EXPERT * CTX, QDIM).astype(jnp.bfloat16)


def draw_queries(key, part):
    values_all = jnp.clip(jax.random.normal(jax.random.fold_in(key, 5), (N_EXPERT, TOK_GRP, HEADS, QDIM), jnp.float32), -5.0, 5.0)
    return values_all.reshape(TOKENS, HEADS, QDIM).astype(jnp.bfloat16)


def steps_of(rng, shape, shards, low, top_value):
    factor_of = 1.0
    for dim, shards_of in shards:
        draws = jax.random.uniform(jax.random.fold_in(jax.random.fold_in(rng, 6), dim), (shards_of,), jnp.float32, low / len(shards), top_value / len(shards))
        factor_of = factor_of * jnp.repeat(jnp.exp(draws), shape[dim] // shards_of).reshape((-1,) + (1,) * (len(shape) - 1 - dim))
    return factor_of


def shared_out(key, own, number, rows, number_of, top, limit, slope):
    sequence = jax.random.permutation(key, number_of)
    crowded, common = portions_of(number_of, rows * top, limit, slope, True), portions_of(number_of, rows * top, limit, slope, False)
    places = jnp.arange(number_of)

    def named(tallies, turn):
        used = int((tallies > 0).sum())
        fixed = max(1, used // 4)
        shifted = fixed + (places - fixed + turn * (used - fixed)) % max(1, number_of - fixed)
        return jnp.zeros((number_of,), jnp.int32).at[sequence[jnp.where(places < fixed, places, shifted)]].set(jnp.asarray(tallies, jnp.int32))

    tallies = jnp.where(number % 4 == 0, named(crowded, number // 4), named(common, number - number // 4 - 1))
    mixed = jax.random.permutation(jax.random.fold_in(own, 3), number_of)
    giver, taker = mixed[0:number_of // 2 * 2:2], mixed[1:number_of // 2 * 2:2]
    slack = jnp.minimum(tallies[giver] - 1, limit - tallies[taker]) // 2
    slack = jnp.where((giver == sequence[0]) | (taker == sequence[0]) | (tallies[taker] == 0), 0, jnp.maximum(slack, 0))
    shifted = jax.random.randint(jax.random.fold_in(own, 4), (number_of // 2,), 0, 1 << 20) % (slack + 1)
    tallies = tallies.at[giver].add(-shifted).at[taker].add(shifted)
    items = jnp.searchsorted(jnp.cumsum(tallies), jnp.arange(rows * top), side="right").astype(jnp.int32)
    listing = items.reshape(top, rows).T
    listing = listing[jax.random.permutation(jax.random.fold_in(own, 1), rows)]
    turn = jax.random.randint(jax.random.fold_in(own, 2), (rows, 1), 0, top)
    return jnp.take_along_axis(listing, (jnp.arange(top)[None, :] + turn) % top, axis=1)


def portions_of(amount, total, bound, lean, full):
    loads = [(1 << 20) // math.isqrt(rank ** lean) + 1 for rank in range(1, amount + 1)]
    largest = bound if full else min(bound, max(-(-total // amount), total * loads[0] // sum(loads)))
    least = 1 if total - largest >= amount - 1 else 0
    holding, rest = [largest] + [least] * (amount - 1), total - largest - least * (amount - 1)
    while rest > 0:
        free = [i for i in range(1, amount) if holding[i] < largest] or [i for i in range(1, amount) if holding[i] < bound]
        pool, budget = sum([loads[i] for i in free]), rest
        for i in free:
            extra = min(bound - holding[i], max(1, budget * loads[i] // pool), rest)
            holding[i] = holding[i] + extra
            rest = rest - extra
    return np.array(holding)


def gaussian(own_key, extent, scale, most, cuts=(), held_as=jnp.bfloat16):
    array = scale * jax.random.normal(own_key, extent, jnp.float32)
    if cuts:
        array = array * steps_of(own_key, extent, cuts, -0.22, 0.18)
    return jnp.clip(array, -most, most).astype(held_as)


def setup_inputs(seed: int = 0) -> dict:
    streams_of = jax.random.split(jax.random.key(seed), 13)
    queries = draw_queries(jax.random.fold_in(streams_of[12], 71), 0)
    latent_cache = draw_latent_cache(jax.random.fold_in(streams_of[12], 71), 0)
    new_latents = gaussian(streams_of[2], (TOKENS, QDIM), 1.0, 5.0, ((0, 8),))
    residual = gaussian(streams_of[3], (TOKENS, D), 1.0, 6.0, ((0, 32),))
    w_uv = gaussian(streams_of[4], (HEADS * LATENT, VDIM), LATENT ** -0.5, 0.25, ((0, 32),))
    w_out = gaussian(streams_of[5], (HEADS * VDIM, D), (HEADS * VDIM) ** -0.5, 0.0625, ((0, 32),))
    norm_gain = jnp.clip(1.0 + 0.15 * jax.random.normal(streams_of[6], (D,), jnp.float32), 0.25, 1.75)
    expert_ids_keys = jax.random.split(jax.random.fold_in(streams_of[7], 1), TOKENS // TOK_GRP)
    expert_ids_turns = jax.random.permutation(jax.random.fold_in(streams_of[7], 3), TOKENS // TOK_GRP)
    expert_ids = jax.vmap(lambda own, number: shared_out(jax.random.fold_in(streams_of[7], 2), own, number, TOK_GRP, EXPERTS, TOP, CAP, 2))(expert_ids_keys, expert_ids_turns).reshape((TOKENS, TOP))
    gate_weights = jnp.clip(0.1 + 0.5 * jax.random.uniform(streams_of[8], (TOKENS, TOP), jnp.float32) ** steps_of(streams_of[8], (TOKENS, TOP), ((0, 8),), -0.2, 0.2), 0.1, 0.6)
    w_gate = gaussian(streams_of[9], (EXPERTS, D, FF), D ** -0.5, 0.09375, ((0, 8), (2, 4)))
    w_up = gaussian(streams_of[10], (EXPERTS, D, FF), D ** -0.5, 0.09375, ((0, 8), (2, 4)))
    w_down = gaussian(streams_of[11], (EXPERTS, FF, D), FF ** -0.5, 0.1875, ((0, 8), (1, 4)))
    return dict(queries=queries, latent_cache=latent_cache, new_latents=new_latents, residual=residual, w_uv=w_uv, w_out=w_out, norm_gain=norm_gain, expert_ids=expert_ids, gate_weights=gate_weights, w_gate=w_gate, w_up=w_up, w_down=w_down)


EPSILON = 1e-06

def route_slots(route_ids):
    onehot = (route_ids[:, None] == jnp.arange(EXPERTS, dtype=jnp.int32)[None, :]).astype(jnp.int32)
    before = jnp.cumsum(onehot, axis=0) - onehot
    return lax.optimization_barrier(jnp.sum(before * onehot, axis=1)).astype(jnp.int32)

def reference(queries, latent_cache, new_latents, residual, w_uv, w_out, norm_gain, expert_ids, gate_weights, w_gate, w_up, w_down):
    uv_heads = w_uv.reshape(HEADS, LATENT, VDIM).astype(jnp.float32)
    score_scale = (VDIM + ROPE) ** (-0.5)

    def attend_group(inputs):
        group_q, group_cache, group_new = inputs
        key_rows = jnp.concatenate([group_cache, group_new], axis=0)
        scores = jnp.einsum('thc,kc->htk', group_q.astype(jnp.float32), key_rows.astype(jnp.float32)) * score_scale
        query_pos = jnp.arange(TOK_GRP, dtype=jnp.int32)[:, None]
        key_pos = jnp.arange(CTX + TOK_GRP, dtype=jnp.int32)[None, :] - CTX
        scores = jnp.where((key_pos <= query_pos)[None], scores, -jnp.inf)
        row_peak = lax.optimization_barrier(jnp.max(scores, axis=2, keepdims=True))
        exp_scores = jnp.exp(scores - row_peak)
        attn_probs = (exp_scores / lax.optimization_barrier(jnp.sum(exp_scores, axis=2, keepdims=True))).astype(jnp.bfloat16)
        attended = jnp.einsum('htk,kl->thl', attn_probs.astype(jnp.float32), key_rows[:, :LATENT].astype(jnp.float32)).astype(jnp.bfloat16)
        head_values = jnp.einsum('thl,hlv->thv', attended.astype(jnp.float32), uv_heads).astype(jnp.bfloat16)
        return head_values
    head_values = lax.map(attend_group, (queries.reshape(N_EXPERT, TOK_GRP, HEADS, QDIM), latent_cache.reshape(N_EXPERT, CTX, QDIM), new_latents.reshape(N_EXPERT, TOK_GRP, QDIM)))
    attn_out = jnp.dot(head_values.reshape(TOKENS, HEADS * VDIM), w_out, preferred_element_type=jnp.float32)
    hidden = residual.astype(jnp.float32) + attn_out
    scale_rows = lax.rsqrt(lax.optimization_barrier(jnp.mean(hidden * hidden, axis=1, keepdims=True)) + EPSILON)
    normed = (hidden * scale_rows * norm_gain).astype(jnp.bfloat16)
    grouped_ids = expert_ids.reshape(N_EXPERT, TOK_GRP * TOP)
    slots = jax.vmap(route_slots)(grouped_ids)
    group_index = jnp.arange(N_EXPERT, dtype=jnp.int32)[:, None]
    slot_index = (grouped_ids * (N_EXPERT * CAP) + group_index * CAP + slots).reshape(-1)
    source = jnp.arange(TOKENS * TOP, dtype=jnp.int32) // TOP
    buffer_rows = jnp.zeros((EXPERTS * N_EXPERT * CAP, D), jnp.bfloat16).at[slot_index].set(jnp.take(normed, source, axis=0))

    def expert_rows(inputs):
        rows_in, gate_mat, up_mat, down_mat = inputs
        gate_part = jnp.dot(rows_in, gate_mat, preferred_element_type=jnp.float32)
        up_part = jnp.dot(rows_in, up_mat, preferred_element_type=jnp.float32)
        active = (jax.nn.silu(gate_part) * up_part).astype(jnp.bfloat16)
        active = lax.optimization_barrier(active)
        pieces = jnp.einsum('rsf,sfd->rsd', active.reshape(-1, N_TENSOR, FF // N_TENSOR).astype(jnp.float32), down_mat.reshape(N_TENSOR, FF // N_TENSOR, D).astype(jnp.float32))
        slice_out = lax.optimization_barrier(pieces.astype(jnp.bfloat16))
        return lax.optimization_barrier(jnp.sum(slice_out.astype(jnp.float32), axis=1))
    expert_out = lax.map(expert_rows, (buffer_rows.reshape(EXPERTS, N_EXPERT * CAP, D), w_gate, w_up, w_down))
    routed = jnp.take(expert_out.reshape(EXPERTS * N_EXPERT * CAP, D), slot_index, axis=0)
    mixed_sum = lax.optimization_barrier(jnp.sum((routed * gate_weights.reshape(-1, 1)).reshape(TOKENS, TOP, D), axis=1))
    return (hidden + mixed_sum).astype(jnp.bfloat16)
```

```python
import jax
import jax.numpy as jnp
from jax import lax
from jax.sharding import PartitionSpec as P

LATENT = 512
ROPE = 64
VDIM = 128


EPSILON = 1e-06


def rms_rows(rows, norm_gain):
    scale_rows = lax.rsqrt(jnp.mean(rows * rows, axis=1, keepdims=True) + EPSILON)
    return (rows * scale_rows * norm_gain).astype(jnp.bfloat16)


def attend(queries, latent_cache, new_latents):
    tok_rows = queries.shape[0]
    context = latent_cache.shape[0]
    key_rows = jnp.concatenate([latent_cache, new_latents], axis=0)
    scores = jnp.einsum("thc,kc->htk", queries, key_rows, preferred_element_type=jnp.float32) * (
        VDIM + ROPE
    ) ** (-0.5)
    query_pos = jnp.arange(tok_rows, dtype=jnp.int32)[:, None]
    key_pos = jnp.arange(key_rows.shape[0], dtype=jnp.int32)[None, :] - context
    scores = jnp.where((key_pos <= query_pos)[None], scores, -jnp.inf)
    row_peak = jnp.max(scores, axis=2, keepdims=True)
    exp_scores = jnp.exp(scores - row_peak)
    attn_probs = (exp_scores / jnp.sum(exp_scores, axis=2, keepdims=True)).astype(jnp.bfloat16)
    return jnp.einsum(
        "htk,kl->htl", attn_probs, key_rows[:, :LATENT], preferred_element_type=jnp.float32
    ).astype(jnp.bfloat16)


def per_device(
    queries,
    latent_cache,
    new_latents,
    residual,
    w_uv,
    w_out,
    norm_gain,
    expert_ids,
    gate_weights,
    w_gate,
    w_up,
    w_down,
):
    group_count = lax.axis_size("expert")
    tok_rows = queries.shape[0]
    head_count = queries.shape[1]
    local_experts = w_gate.shape[0]
    experts_all = local_experts * group_count
    everyone = ("expert", "tensor")

    chosen = expert_ids[:, :, None] == jnp.arange(experts_all, dtype=jnp.int32)
    mix = jnp.sum(jnp.where(chosen, gate_weights[:, :, None], 0.0), axis=1)
    mix = lax.all_to_all(
        mix.reshape(tok_rows, group_count, local_experts),
        "expert",
        split_axis=1,
        concat_axis=0,
        tiled=True,
    ).reshape(-1, local_experts)

    uv_rows = lax.all_gather(w_uv, "expert", axis=0, tiled=True)
    attended = attend(queries, latent_cache, new_latents)
    head_values = jnp.einsum(
        "htl,hlv->thv",
        attended,
        uv_rows.reshape(head_count, LATENT, VDIM),
        preferred_element_type=jnp.float32,
    ).astype(jnp.bfloat16)
    columns = head_values.reshape(tok_rows, group_count, -1)
    columns = lax.all_to_all(columns, "expert", split_axis=1, concat_axis=0, tiled=True)
    columns = columns.reshape(group_count * tok_rows, -1)
    share = jnp.dot(columns, w_out, preferred_element_type=jnp.float32).astype(jnp.bfloat16)
    own_hidden = lax.psum_scatter(share, everyone, scatter_dimension=0, tiled=True).astype(
        jnp.float32
    ) + residual.astype(jnp.float32)
    normed = lax.all_gather(rms_rows(own_hidden, norm_gain), everyone, axis=0, tiled=True)

    gate_part = jnp.einsum("nd,edf->enf", normed, w_gate, preferred_element_type=jnp.float32)
    up_part = jnp.einsum("nd,edf->enf", normed, w_up, preferred_element_type=jnp.float32)
    active = (jax.nn.silu(gate_part) * up_part * mix.T[:, :, None]).astype(jnp.bfloat16)
    produced = jnp.einsum("enf,efd->nd", active, w_down, preferred_element_type=jnp.float32)
    summed = lax.psum_scatter(
        produced.astype(jnp.bfloat16), everyone, scatter_dimension=0, tiled=True
    ).astype(jnp.float32)
    return (own_hidden + summed).astype(jnp.bfloat16)


def solution(mesh):
    placed = (
        P("expert", "tensor", None),
        P("expert", None),
        P("expert", None),
        P(("expert", "tensor"), None),
        P(("tensor", "expert"), None),
        P(("tensor", "expert"), None),
        P(),
        P("expert", None),
        P("expert", None),
        P("expert", None, "tensor"),
        P("expert", None, "tensor"),
        P("expert", "tensor", None),
    )
    return jax.shard_map(
        per_device,
        mesh=mesh,
        in_specs=placed,
        out_specs=P(("expert", "tensor"), None),
        check_vma=False,
    )
```

```python
import functools

import jax
import jax.numpy as jnp
from jax import lax
from jax.experimental import pallas as pl
from jax.experimental.pallas import tpu as pltpu
from jax.sharding import PartitionSpec as P

LATENT = 512
ROPE = 64
VDIM = 128


EPSILON = 1e-06


MESH = pl.DeviceIdType.MESH
VMEM_BYTES = 60 * 2**20


def stage_orders(experts_n, tensor_n):
    e_bits = [("expert", 1 << k) for k in range(experts_n.bit_length() - 1)]
    t_bits = [("tensor", 1 << k) for k in range(tensor_n.bit_length() - 1)]
    core, plane = e_bits[:1], e_bits[1:]
    return (
        core + plane + t_bits,
        core + plane[1:] + t_bits + plane[:1],
        core + t_bits + plane,
    )


def piece_columns(width, count):
    units = width // 256
    sizes = [(units + count - 1 - i) // count * 256 for i in range(count)]
    sizes[0] += width - sum(sizes)
    return [(sum(sizes[:i]), sizes[i]) for i in range(count)]


def natural_dim(stage, experts_n, tensor_n):
    axis, stride = stage
    e_bits, t_bits = experts_n.bit_length() - 1, tensor_n.bit_length() - 1
    last = e_bits if axis == "expert" else e_bits + t_bits
    return last - stride.bit_length()


def in_order(rows, order, experts_n, tensor_n):
    bits = len(order)
    block = rows.shape[0] >> bits
    split = rows.reshape((2,) * bits + (block, rows.shape[1]))
    dims = [natural_dim(s, experts_n, tensor_n) for s in order]
    return split.transpose(dims + [bits, bits + 1]).reshape(rows.shape)


def my_bit(stage):
    return lax.rem(lax.axis_index(stage[0]) // stage[1], 2)


def partner(stage):
    axis, stride = stage
    return {axis: lax.axis_index(axis) + stride * (1 - 2 * my_bit(stage))}


def greet(stages):
    barrier = pltpu.get_barrier_semaphore()
    for stage in stages:
        pl.semaphore_signal(barrier, inc=1, device_id=partner(stage), device_id_type=MESH)
    pl.semaphore_wait(barrier, len(stages))


def project(lhs_ref, w_ref, buf, start):
    blocks, block, width = buf.shape

    @pl.loop(0, width // 256)
    def _(c):
        off = pl.multiple_of(c * 256, 256)
        tile = jnp.dot(
            lhs_ref[...],
            w_ref[:, pl.ds(pl.multiple_of(start + off, 256), 256)],
            preferred_element_type=jnp.float32,
        )
        buf[:, :, pl.ds(off, 256)] = tile.reshape(blocks, block, 256).astype(buf.dtype)


def halve(order, step, low, buf, got, send_sem, recv_sem):
    half = buf.shape[0] >> (step + 1)
    bit = my_bit(order[step])
    at = buf.shape[0] - 2 * half
    copy = pltpu.make_async_remote_copy(
        src_ref=buf.at[pl.ds(low + (1 - bit) * half, half)],
        dst_ref=got.at[pl.ds(at, half)],
        send_sem=send_sem.at[step],
        recv_sem=recv_sem.at[step],
        device_id=partner(order[step]),
        device_id_type=MESH,
    )
    copy.start()
    return copy, low + bit * half


def reduce_scatter(orders, columns, lhs, w_ref, bufs, gots, send_sem, recv_sem, finish):
    count = len(orders)
    held, pending = [], []
    for p in range(count):
        project(lhs[p], w_ref, bufs[p], columns[p][0])
        copy, low = halve(orders[p], 0, 0, bufs[p], gots[p], send_sem.at[p], recv_sem.at[p])
        pending.append(copy)
        held.append(low)
    steps = len(orders[0])
    started = list(pending)
    for step in range(steps):
        for p in range(count):
            pending[p].wait_recv()
            half = bufs[p].shape[0] >> (step + 1)
            at = bufs[p].shape[0] - 2 * half
            if step == steps - 1:
                total = bufs[p][held[p]].astype(jnp.float32) + gots[p][at].astype(jnp.float32)
                finish(p, total)
                continue

            def add(i, _, p=p, at=at, low=held[p]):
                mine = bufs[p][low + i].astype(jnp.float32)
                bufs[p][low + i] = (mine + gots[p][at + i].astype(jnp.float32)).astype(jnp.bfloat16)
                return 0

            lax.fori_loop(0, half, add, 0)
            pending[p], held[p] = halve(
                orders[p], step + 1, held[p], bufs[p], gots[p], send_sem.at[p], recv_sem.at[p]
            )
            started.append(pending[p])
    for copy in started:
        copy.wait_send()


def attention_out_kernel(
    orders, columns, sizes, l0, l1, l2, w_ref, res_ref, gain_ref, hid_ref, all_ref,
    b0, b1, b2, g0, g1, g2, a0, a1, a2, send_sem, recv_sem, ag_send, ag_recv,
):
    greet(orders[0])
    bits = len(orders[0])

    def finish(p, total):
        cols = pl.ds(*columns[p])
        hid_ref[:, cols] = total + res_ref[:, cols].astype(jnp.float32)

    reduce_scatter(
        orders, columns, (l0, l1, l2), w_ref, (b0, b1, b2), (g0, g1, g2), send_sem, recv_sem, finish
    )
    rows = hid_ref[...]
    scale = lax.rsqrt(jnp.mean(rows * rows, axis=1, keepdims=True) + EPSILON)
    held, copies = [], []
    gathered = (a0, a1, a2)
    for p, order in enumerate(orders):
        place = 0
        for stage in order:
            place = place * 2 + my_bit(stage)
        cols = pl.ds(*columns[p])
        gathered[p][place] = (hid_ref[:, cols] * scale * gain_ref[:, cols]).astype(jnp.bfloat16)
        held.append(place)
    for step in range(bits):
        for p, order in enumerate(orders):
            stage = order[bits - 1 - step]
            if step:
                copies[-len(orders)].wait_recv()
            part = gathered[p].at[pl.ds(held[p], 1 << step)]
            copy = pltpu.make_async_remote_copy(
                src_ref=part,
                dst_ref=part,
                send_sem=ag_send.at[p, step],
                recv_sem=ag_recv.at[p, step],
                device_id=partner(stage),
                device_id_type=MESH,
            )
            copy.start()
            copies.append(copy)
            held[p] = held[p] - my_bit(stage) * (1 << step)
    for p, order in enumerate(orders):
        copies[p - len(orders)].wait_recv()

        def place_block(i, _, p=p, order=order):
            natural = 0
            for k, stage in enumerate(order):
                dim = natural_dim(stage, *sizes)
                natural = natural + lax.rem(i // (1 << (bits - 1 - k)), 2) * (1 << (bits - 1 - dim))
            all_ref[natural, :, pl.ds(*columns[p])] = gathered[p][i]
            return 0

        lax.fori_loop(0, 1 << bits, place_block, 0)
    for copy in copies:
        copy.wait_send()


def down_kernel(
    orders, columns, l0, l1, l2, w_ref, hid_ref, out_ref, b0, b1, b2, g0, g1, g2, send_sem, recv_sem
):
    greet(orders[0])

    def finish(p, total):
        cols = pl.ds(*columns[p])
        out_ref[:, cols] = (hid_ref[:, cols] + total).astype(out_ref.dtype)

    reduce_scatter(
        orders, columns, (l0, l1, l2), w_ref, (b0, b1, b2), (g0, g1, g2), send_sem, recv_sem, finish
    )


def call(kernel, collective_id, args, outs, blocks, block, columns, gathers, steps, cost):
    vmem = pl.BlockSpec(memory_space=pltpu.VMEM)
    bufs = [pltpu.VMEM((blocks, block, w), jnp.bfloat16) for _, w in columns]
    sems = [pltpu.SemaphoreType.DMA((len(columns), steps))] * (4 if gathers else 2)
    return pl.pallas_call(
        kernel,
        out_shape=outs,
        in_specs=[vmem] * len(args),
        out_specs=jax.tree.map(lambda _: vmem, outs),
        scratch_shapes=bufs * (3 if gathers else 2) + sems,
        compiler_params=pltpu.CompilerParams(
            collective_id=collective_id, has_side_effects=True, vmem_limit_bytes=VMEM_BYTES
        ),
        cost_estimate=cost,
    )(*args)


def attend(queries, latent_cache, new_latents):
    tok_rows = queries.shape[0]
    context = latent_cache.shape[0]
    key_rows = jnp.concatenate([latent_cache, new_latents], axis=0)
    scores = jnp.einsum("thc,kc->htk", queries, key_rows, preferred_element_type=jnp.float32) * (
        VDIM + ROPE
    ) ** (-0.5)
    query_pos = jnp.arange(tok_rows, dtype=jnp.int32)[:, None]
    key_pos = jnp.arange(key_rows.shape[0], dtype=jnp.int32)[None, :] - context
    scores = jnp.where((key_pos <= query_pos)[None], scores, -jnp.inf)
    row_peak = jnp.max(scores, axis=2, keepdims=True)
    exp_scores = jnp.exp(scores - row_peak)
    attn_probs = (exp_scores / jnp.sum(exp_scores, axis=2, keepdims=True)).astype(jnp.bfloat16)
    return jnp.einsum(
        "htk,kl->htl", attn_probs, key_rows[:, :LATENT], preferred_element_type=jnp.float32
    ).astype(jnp.bfloat16)


def per_device(
    queries,
    latent_cache,
    new_latents,
    residual,
    w_uv,
    w_out,
    norm_gain,
    expert_ids,
    gate_weights,
    w_gate,
    w_up,
    w_down,
):
    group_count = lax.axis_size("expert")
    tok_rows = queries.shape[0]
    head_count = queries.shape[1]
    local_experts = w_gate.shape[0]
    experts_all = local_experts * group_count
    everyone = ("expert", "tensor")

    chosen = expert_ids[:, :, None] == jnp.arange(experts_all, dtype=jnp.int32)
    mix = jnp.sum(jnp.where(chosen, gate_weights[:, :, None], 0.0), axis=1)
    mix = lax.all_to_all(
        mix.reshape(tok_rows, group_count, local_experts),
        "expert",
        split_axis=1,
        concat_axis=0,
        tiled=True,
    ).reshape(-1, local_experts)

    uv_rows = lax.all_gather(w_uv, "expert", axis=0, tiled=True)
    attended = attend(queries, latent_cache, new_latents)
    head_values = jnp.einsum(
        "htl,hlv->thv",
        attended,
        uv_rows.reshape(head_count, LATENT, VDIM),
        preferred_element_type=jnp.float32,
    ).astype(jnp.bfloat16)
    columns = head_values.reshape(tok_rows, group_count, -1)
    columns = lax.all_to_all(columns, "expert", split_axis=1, concat_axis=0, tiled=True)
    columns = columns.reshape(group_count * tok_rows, -1)
    tensor_n = lax.axis_size("tensor")
    sizes = (group_count, tensor_n)
    orders = stage_orders(*sizes)
    model_width = residual.shape[1]
    cut = piece_columns(model_width, len(orders))
    blocks = group_count * tensor_n
    block = residual.shape[0]
    steps = len(orders[0])
    flops = 2 * blocks * block * w_out.size
    own_hidden, normed = call(
        functools.partial(attention_out_kernel, orders, cut, sizes),
        0,
        [in_order(columns, o, *sizes) for o in orders]
        + [w_out, residual, norm_gain.reshape(1, model_width)],
        (
            jax.ShapeDtypeStruct((block, model_width), jnp.float32),
            jax.ShapeDtypeStruct((blocks, block, model_width), jnp.bfloat16),
        ),
        blocks,
        block,
        cut,
        True,
        steps,
        pl.CostEstimate(flops=flops, bytes_accessed=w_out.size * 2, transcendentals=0),
    )
    normed = normed.reshape(blocks * block, model_width)

    gate_part = jnp.einsum("nd,edf->nef", normed, w_gate, preferred_element_type=jnp.float32)
    up_part = jnp.einsum("nd,edf->nef", normed, w_up, preferred_element_type=jnp.float32)
    active = (jax.nn.silu(gate_part) * up_part * mix[:, :, None]).astype(jnp.bfloat16)
    active = active.reshape(blocks * block, -1)
    return call(
        functools.partial(down_kernel, orders, cut),
        1,
        [in_order(active, o, *sizes) for o in orders] + [w_down.reshape(-1, model_width), own_hidden],
        jax.ShapeDtypeStruct((block, model_width), jnp.bfloat16),
        blocks,
        block,
        cut,
        False,
        steps,
        pl.CostEstimate(flops=2 * blocks * block * w_down.size, bytes_accessed=w_down.size * 2, transcendentals=0),
    )


def solution(mesh):
    placed = (
        P("expert", "tensor", None),
        P("expert", None),
        P("expert", None),
        P(("expert", "tensor"), None),
        P(("tensor", "expert"), None),
        P(("tensor", "expert"), None),
        P(),
        P("expert", None),
        P("expert", None),
        P("expert", None, "tensor"),
        P("expert", None, "tensor"),
        P("expert", "tensor", None),
    )
    return jax.shard_map(
        per_device,
        mesh=mesh,
        in_specs=placed,
        out_specs=P(("expert", "tensor"), None),
        check_vma=False,
    )
```

```python
import functools

import jax
import jax.numpy as jnp
from jax import lax
from jax.experimental import pallas as pl
from jax.experimental.pallas import tpu as pltpu
from jax.sharding import PartitionSpec as P

LATENT = 512
ROPE = 64
VDIM = 128


EPSILON = 1e-06


MESH = pl.DeviceIdType.MESH
VMEM_BYTES = 60 * 2**20


def stage_orders(experts_n, tensor_n):
    e_bits = [("expert", 1 << k) for k in range(experts_n.bit_length() - 1)]
    t_bits = [("tensor", 1 << k) for k in range(tensor_n.bit_length() - 1)]
    core, plane = e_bits[:1], e_bits[1:]
    return (
        core + plane + t_bits,
        core + plane[1:] + t_bits + plane[:1],
        core + t_bits + plane,
    ) * 2


def piece_columns(width, count):
    units = width // 256
    sizes = [(units + count - 1 - i) // count * 256 for i in range(count)]
    sizes[0] += width - sum(sizes)
    return [(sum(sizes[:i]), sizes[i]) for i in range(count)]


def natural_dim(stage, experts_n, tensor_n):
    axis, stride = stage
    e_bits, t_bits = experts_n.bit_length() - 1, tensor_n.bit_length() - 1
    last = e_bits if axis == "expert" else e_bits + t_bits
    return last - stride.bit_length()


def in_order(rows, order, experts_n, tensor_n):
    bits = len(order)
    block = rows.shape[0] >> bits
    split = rows.reshape((2,) * bits + (block, rows.shape[1]))
    dims = [natural_dim(s, experts_n, tensor_n) for s in order]
    return split.transpose(dims + [bits, bits + 1]).reshape(rows.shape)


def my_bit(stage):
    return lax.rem(lax.axis_index(stage[0]) // stage[1], 2)


def partner(stage):
    axis, stride = stage
    return {axis: lax.axis_index(axis) + stride * (1 - 2 * my_bit(stage))}


def greet(stages):
    barrier = pltpu.get_barrier_semaphore()
    for stage in stages:
        pl.semaphore_signal(barrier, inc=1, device_id=partner(stage), device_id_type=MESH)
    pl.semaphore_wait(barrier, len(stages))


def project(lhs_ref, w_ref, buf, start):
    blocks, block, width = buf.shape

    @pl.loop(0, width // 256)
    def _(c):
        off = pl.multiple_of(c * 256, 256)
        tile = jnp.dot(
            lhs_ref[...],
            w_ref[:, pl.ds(pl.multiple_of(start + off, 256), 256)],
            preferred_element_type=jnp.float32,
        )
        buf[:, :, pl.ds(off, 256)] = tile.reshape(blocks, block, 256).astype(buf.dtype)


def halve(order, step, low, buf, got, send_sem, recv_sem):
    half = buf.shape[0] >> (step + 1)
    bit = my_bit(order[step])
    at = buf.shape[0] - 2 * half
    copy = pltpu.make_async_remote_copy(
        src_ref=buf.at[pl.ds(low + (1 - bit) * half, half)],
        dst_ref=got.at[pl.ds(at, half)],
        send_sem=send_sem.at[step],
        recv_sem=recv_sem.at[step],
        device_id=partner(order[step]),
        device_id_type=MESH,
    )
    copy.start()
    return copy, low + bit * half


def reduce_scatter(orders, columns, lhs, w_ref, bufs, gots, send_sem, recv_sem, finish):
    count = len(orders)
    held, pending = [], []
    for p in range(count):
        project(lhs[p % len(lhs)], w_ref, bufs[p], columns[p][0])
        copy, low = halve(orders[p], 0, 0, bufs[p], gots[p], send_sem.at[p], recv_sem.at[p])
        pending.append(copy)
        held.append(low)
    steps = len(orders[0])
    started = list(pending)
    for step in range(steps):
        for p in range(count):
            pending[p].wait_recv()
            half = bufs[p].shape[0] >> (step + 1)
            at = bufs[p].shape[0] - 2 * half
            if step == steps - 1:
                total = bufs[p][held[p]].astype(jnp.float32) + gots[p][at].astype(jnp.float32)
                finish(p, total)
                continue

            def add(i, _, p=p, at=at, low=held[p]):
                mine = bufs[p][low + i].astype(jnp.float32)
                bufs[p][low + i] = (mine + gots[p][at + i].astype(jnp.float32)).astype(jnp.bfloat16)
                return 0

            lax.fori_loop(0, half, add, 0)
            pending[p], held[p] = halve(
                orders[p], step + 1, held[p], bufs[p], gots[p], send_sem.at[p], recv_sem.at[p]
            )
            started.append(pending[p])
    for copy in started:
        copy.wait_send()


def attention_out_kernel(orders, columns, sizes, *refs):
    count = len(orders)
    lhs, refs = refs[: count // 2], refs[count // 2 :]
    w_ref, res_ref, gain_ref, mix_ref, hid_ref, all_ref, mix_all_ref = refs[:7]
    bufs, gots, gathered = (refs[7 + i * count : 7 + (i + 1) * count] for i in range(3))
    send_sem, recv_sem, ag_send, ag_recv = refs[7 + 3 * count :]
    greet(orders[0])
    bits = len(orders[0])

    def finish(p, total):
        cols = pl.ds(*columns[p])
        hid_ref[:, cols] = total + res_ref[:, cols].astype(jnp.float32)

    reduce_scatter(orders, columns, lhs, w_ref, bufs, gots, send_sem, recv_sem, finish)
    rows = hid_ref[...]
    scale = lax.rsqrt(jnp.mean(rows * rows, axis=1, keepdims=True) + EPSILON)
    held, copies = [], []
    for p, order in enumerate(orders):
        place = 0
        for stage in order:
            place = place * 2 + my_bit(stage)
        cols = pl.ds(*columns[p])
        wide = columns[p][1]
        gathered[p][place, :, :wide] = (hid_ref[:, cols] * scale * gain_ref[:, cols]).astype(
            jnp.bfloat16
        )
        if p == count - 1:
            gathered[p][place, :, wide:] = mix_ref[...]
        held.append(place)
    for step in range(bits):
        for p, order in enumerate(orders):
            stage = order[bits - 1 - step]
            if step:
                copies[-len(orders)].wait_recv()
            part = gathered[p].at[pl.ds(held[p], 1 << step)]
            copy = pltpu.make_async_remote_copy(
                src_ref=part,
                dst_ref=part,
                send_sem=ag_send.at[p, step],
                recv_sem=ag_recv.at[p, step],
                device_id=partner(stage),
                device_id_type=MESH,
            )
            copy.start()
            copies.append(copy)
            held[p] = held[p] - my_bit(stage) * (1 << step)
    for p, order in enumerate(orders):
        copies[p - len(orders)].wait_recv()

        def place_block(i, _, p=p, order=order):
            natural = 0
            for k, stage in enumerate(order):
                dim = natural_dim(stage, *sizes)
                natural = natural + lax.rem(i // (1 << (bits - 1 - k)), 2) * (1 << (bits - 1 - dim))
            wide = columns[p][1]
            all_ref[natural, :, pl.ds(*columns[p])] = gathered[p][i, :, :wide]
            if p == count - 1:
                mix_all_ref[natural] = gathered[p][i, :, wide:]
            return 0

        lax.fori_loop(0, 1 << bits, place_block, 0)
    for copy in copies:
        copy.wait_send()


def down_kernel(orders, columns, *refs):
    count = len(orders)
    lhs, refs = refs[: count // 2], refs[count // 2 :]
    w_ref, hid_ref, out_ref = refs[:3]
    bufs, gots = refs[3 : 3 + count], refs[3 + count : 3 + 2 * count]
    send_sem, recv_sem = refs[3 + 2 * count :]
    greet(orders[0])

    def finish(p, total):
        cols = pl.ds(*columns[p])
        out_ref[:, cols] = (hid_ref[:, cols] + total).astype(out_ref.dtype)

    reduce_scatter(orders, columns, lhs, w_ref, bufs, gots, send_sem, recv_sem, finish)


def call(kernel, collective_id, args, outs, blocks, block, columns, extra, steps, cost):
    vmem = pl.BlockSpec(memory_space=pltpu.VMEM)
    bufs = [pltpu.VMEM((blocks, block, w), jnp.bfloat16) for _, w in columns]
    sems = [pltpu.SemaphoreType.DMA((len(columns), steps))] * (4 if extra else 2)
    wider = [w for _, w in columns[:-1]] + [columns[-1][1] + extra]
    gathered = [pltpu.VMEM((blocks, block, w), jnp.bfloat16) for w in wider] if extra else []
    return pl.pallas_call(
        kernel,
        out_shape=outs,
        in_specs=[vmem] * len(args),
        out_specs=jax.tree.map(lambda _: vmem, outs),
        scratch_shapes=bufs * 2 + gathered + sems,
        compiler_params=pltpu.CompilerParams(
            collective_id=collective_id, has_side_effects=True, vmem_limit_bytes=VMEM_BYTES
        ),
        cost_estimate=cost,
    )(*args)


def attend(queries, latent_cache, new_latents):
    tok_rows = queries.shape[0]
    context = latent_cache.shape[0]
    key_rows = jnp.concatenate([latent_cache, new_latents], axis=0)
    scores = jnp.einsum("thc,kc->htk", queries, key_rows, preferred_element_type=jnp.float32) * (
        VDIM + ROPE
    ) ** (-0.5)
    query_pos = jnp.arange(tok_rows, dtype=jnp.int32)[:, None]
    key_pos = jnp.arange(key_rows.shape[0], dtype=jnp.int32)[None, :] - context
    scores = jnp.where((key_pos <= query_pos)[None], scores, -jnp.inf)
    row_peak = jnp.max(scores, axis=2, keepdims=True)
    exp_scores = jnp.exp(scores - row_peak)
    attn_probs = (exp_scores / jnp.sum(exp_scores, axis=2, keepdims=True)).astype(jnp.bfloat16)
    return jnp.einsum(
        "htk,kl->htl", attn_probs, key_rows[:, :LATENT], preferred_element_type=jnp.float32
    ).astype(jnp.bfloat16)


def per_device(
    queries,
    latent_cache,
    new_latents,
    residual,
    w_uv,
    w_out,
    norm_gain,
    expert_ids,
    gate_weights,
    w_gate,
    w_up,
    w_down,
):
    group_count = lax.axis_size("expert")
    tok_rows = queries.shape[0]
    head_count = queries.shape[1]
    local_experts = w_gate.shape[0]
    experts_all = local_experts * group_count

    block = residual.shape[0]
    first = lax.axis_index("tensor") * block
    own_ids = lax.dynamic_slice_in_dim(expert_ids, first, block, 0)
    own_weights = lax.dynamic_slice_in_dim(gate_weights, first, block, 0)
    chosen = own_ids[:, :, None] == jnp.arange(experts_all, dtype=jnp.int32)
    mix = jnp.sum(jnp.where(chosen, own_weights[:, :, None], 0.0), axis=1)
    high = lax.reduce_precision(mix, 8, 7)
    extra = -(-2 * experts_all // 128) * 128
    parts = jnp.concatenate([high, mix - high], axis=1).astype(jnp.bfloat16)
    parts = jnp.pad(parts, ((0, 0), (0, extra - 2 * experts_all)))

    attended = attend(queries, latent_cache, new_latents)
    if w_uv.shape[0] % LATENT == 0:
        attended = lax.all_to_all(attended, "expert", split_axis=0, concat_axis=0, tiled=True)
        own_heads = w_uv.shape[0] // LATENT
        columns = jnp.einsum(
            "ghtl,hlv->gthv",
            attended.reshape(group_count, own_heads, tok_rows, LATENT),
            w_uv.reshape(own_heads, LATENT, VDIM),
            preferred_element_type=jnp.float32,
        ).astype(jnp.bfloat16)
    else:
        uv_rows = lax.all_gather(w_uv, "expert", axis=0, tiled=True)
        head_values = jnp.einsum(
            "htl,hlv->thv",
            attended,
            uv_rows.reshape(head_count, LATENT, VDIM),
            preferred_element_type=jnp.float32,
        ).astype(jnp.bfloat16)
        columns = head_values.reshape(tok_rows, group_count, -1)
        columns = lax.all_to_all(columns, "expert", split_axis=1, concat_axis=0, tiled=True)
    columns = columns.reshape(group_count * tok_rows, -1)
    tensor_n = lax.axis_size("tensor")
    sizes = (group_count, tensor_n)
    orders = stage_orders(*sizes)
    model_width = residual.shape[1]
    cut = piece_columns(model_width, len(orders))
    blocks = group_count * tensor_n
    steps = len(orders[0])
    flops = 2 * blocks * block * w_out.size
    own_hidden, normed, mix_all = call(
        functools.partial(attention_out_kernel, orders, cut, sizes),
        0,
        [in_order(columns, o, *sizes) for o in orders[: len(orders) // 2]]
        + [w_out, residual, norm_gain.reshape(1, model_width), parts],
        (
            jax.ShapeDtypeStruct((block, model_width), jnp.float32),
            jax.ShapeDtypeStruct((blocks, block, model_width), jnp.bfloat16),
            jax.ShapeDtypeStruct((blocks, block, extra), jnp.bfloat16),
        ),
        blocks,
        block,
        cut,
        extra,
        steps,
        pl.CostEstimate(flops=flops, bytes_accessed=w_out.size * 2, transcendentals=0),
    )
    normed = normed.reshape(blocks * block, model_width)
    mix_all = mix_all.reshape(blocks * block, extra).astype(jnp.float32)
    mix_all = mix_all[:, :experts_all] + mix_all[:, experts_all : 2 * experts_all]
    mine = lax.axis_index("expert") * local_experts
    mix = lax.dynamic_slice_in_dim(mix_all, mine, local_experts, 1)

    gate_part = jnp.einsum("nd,edf->nef", normed, w_gate, preferred_element_type=jnp.float32)
    up_part = jnp.einsum("nd,edf->nef", normed, w_up, preferred_element_type=jnp.float32)
    active = (jax.nn.silu(gate_part) * up_part * mix[:, :, None]).astype(jnp.bfloat16)
    active = active.reshape(blocks * block, -1)
    return call(
        functools.partial(down_kernel, orders, cut),
        1,
        [in_order(active, o, *sizes) for o in orders[: len(orders) // 2]] + [w_down.reshape(-1, model_width), own_hidden],
        jax.ShapeDtypeStruct((block, model_width), jnp.bfloat16),
        blocks,
        block,
        cut,
        0,
        steps,
        pl.CostEstimate(flops=2 * blocks * block * w_down.size, bytes_accessed=w_down.size * 2, transcendentals=0),
    )


def solution(mesh):
    placed = (
        P("expert", "tensor", None),
        P("expert", None),
        P("expert", None),
        P(("expert", "tensor"), None),
        P(("tensor", "expert"), None),
        P(("tensor", "expert"), None),
        P(),
        P("expert", None),
        P("expert", None),
        P("expert", None, "tensor"),
        P("expert", None, "tensor"),
        P("expert", "tensor", None),
    )
    return jax.shard_map(
        per_device,
        mesh=mesh,
        in_specs=placed,
        out_specs=P(("expert", "tensor"), None),
        check_vma=False,
    )
```

```python
import functools

import jax
import jax.numpy as jnp
from jax import lax
from jax.experimental import pallas as pl
from jax.experimental.pallas import tpu as pltpu
from jax.sharding import PartitionSpec as P

LATENT = 512
ROPE = 64
VDIM = 128


EPSILON = 1e-06


MESH = pl.DeviceIdType.MESH
VMEM_BYTES = 60 * 2**20


def stage_orders(experts_n, tensor_n):
    e_bits = [("expert", 1 << k) for k in range(experts_n.bit_length() - 1)]
    t_bits = [("tensor", 1 << k) for k in range(tensor_n.bit_length() - 1)]
    core, plane = e_bits[:1], e_bits[1:]
    return (
        core + plane + t_bits,
        core + plane[1:] + t_bits + plane[:1],
        core + t_bits + plane,
    ) * 2


def piece_columns(width, count):
    units = width // 256
    sizes = [(units + count - 1 - i) // count * 256 for i in range(count)]
    sizes[0] += width - sum(sizes)
    return [(sum(sizes[:i]), sizes[i]) for i in range(count)]


def natural_dim(stage, experts_n, tensor_n):
    axis, stride = stage
    e_bits, t_bits = experts_n.bit_length() - 1, tensor_n.bit_length() - 1
    last = e_bits if axis == "expert" else e_bits + t_bits
    return last - stride.bit_length()


def in_order(rows, order, experts_n, tensor_n):
    bits = len(order)
    block = rows.shape[0] >> bits
    split = rows.reshape((2,) * bits + (block, rows.shape[1]))
    dims = [natural_dim(s, experts_n, tensor_n) for s in order]
    return split.transpose(dims + [bits, bits + 1]).reshape(rows.shape)


def my_bit(stage):
    return lax.rem(lax.axis_index(stage[0]) // stage[1], 2)


def partner(stage):
    axis, stride = stage
    return {axis: lax.axis_index(axis) + stride * (1 - 2 * my_bit(stage))}


def greet(stages):
    barrier = pltpu.get_barrier_semaphore()
    for stage in stages:
        pl.semaphore_signal(barrier, inc=1, device_id=partner(stage), device_id_type=MESH)
    pl.semaphore_wait(barrier, len(stages))


def project(lhs_ref, w_ref, buf, start):
    blocks, block, width = buf.shape

    @pl.loop(0, width // 256)
    def _(c):
        off = pl.multiple_of(c * 256, 256)
        tile = jnp.dot(
            lhs_ref[...],
            w_ref[:, pl.ds(pl.multiple_of(start + off, 256), 256)],
            preferred_element_type=jnp.float32,
        )
        buf[:, :, pl.ds(off, 256)] = tile.reshape(blocks, block, 256).astype(buf.dtype)


def halve(order, step, low, buf, got, send_sem, recv_sem):
    half = buf.shape[0] >> (step + 1)
    bit = my_bit(order[step])
    at = buf.shape[0] - 2 * half
    copy = pltpu.make_async_remote_copy(
        src_ref=buf.at[pl.ds(low + (1 - bit) * half, half)],
        dst_ref=got.at[pl.ds(at, half)],
        send_sem=send_sem.at[step],
        recv_sem=recv_sem.at[step],
        device_id=partner(order[step]),
        device_id_type=MESH,
    )
    copy.start()
    return copy, low + bit * half


def reduce_scatter(orders, columns, lhs, w_ref, bufs, gots, send_sem, recv_sem, finish):
    count = len(orders)
    held, pending = [], []
    for p in range(count):
        project(lhs[p % len(lhs)], w_ref, bufs[p], columns[p][0])
        copy, low = halve(orders[p], 0, 0, bufs[p], gots[p], send_sem.at[p], recv_sem.at[p])
        pending.append(copy)
        held.append(low)
    steps = len(orders[0])
    started = list(pending)
    for step in range(steps):
        for p in range(count):
            pending[p].wait_recv()
            half = bufs[p].shape[0] >> (step + 1)
            at = bufs[p].shape[0] - 2 * half
            if step == steps - 1:
                total = bufs[p][held[p]].astype(jnp.float32) + gots[p][at].astype(jnp.float32)
                finish(p, total)
                continue

            def add(i, _, p=p, at=at, low=held[p]):
                mine = bufs[p][low + i].astype(jnp.float32)
                bufs[p][low + i] = (mine + gots[p][at + i].astype(jnp.float32)).astype(jnp.bfloat16)
                return 0

            lax.fori_loop(0, half, add, 0)
            pending[p], held[p] = halve(
                orders[p], step + 1, held[p], bufs[p], gots[p], send_sem.at[p], recv_sem.at[p]
            )
            started.append(pending[p])
    for copy in started:
        copy.wait_send()


def attention_out_kernel(orders, columns, sizes, *refs):
    count = len(orders)
    lhs, refs = refs[: count // 2], refs[count // 2 :]
    w_ref, res_ref, gain_ref, mix_ref, hid_ref, all_ref, mix_all_ref = refs[:7]
    bufs, gots, gathered = (refs[7 + i * count : 7 + (i + 1) * count] for i in range(3))
    send_sem, recv_sem, ag_send, ag_recv = refs[7 + 3 * count :]
    greet(orders[0])
    bits = len(orders[0])

    def finish(p, total):
        cols = pl.ds(*columns[p])
        hid_ref[:, cols] = total + res_ref[:, cols].astype(jnp.float32)

    reduce_scatter(orders, columns, lhs, w_ref, bufs, gots, send_sem, recv_sem, finish)
    rows = hid_ref[...]
    scale = lax.rsqrt(jnp.mean(rows * rows, axis=1, keepdims=True) + EPSILON)
    held, copies = [], []
    for p, order in enumerate(orders):
        place = 0
        for stage in order:
            place = place * 2 + my_bit(stage)
        cols = pl.ds(*columns[p])
        wide = columns[p][1]
        gathered[p][place, :, :wide] = (hid_ref[:, cols] * scale * gain_ref[:, cols]).astype(
            jnp.bfloat16
        )
        if p == count - 1:
            gathered[p][place, :, wide:] = mix_ref[...]
        held.append(place)
    for step in range(bits):
        for p, order in enumerate(orders):
            stage = order[bits - 1 - step]
            if step:
                copies[-len(orders)].wait_recv()
            part = gathered[p].at[pl.ds(held[p], 1 << step)]
            copy = pltpu.make_async_remote_copy(
                src_ref=part,
                dst_ref=part,
                send_sem=ag_send.at[p, step],
                recv_sem=ag_recv.at[p, step],
                device_id=partner(stage),
                device_id_type=MESH,
            )
            copy.start()
            copies.append(copy)
            held[p] = held[p] - my_bit(stage) * (1 << step)
    for p, order in enumerate(orders):
        copies[p - len(orders)].wait_recv()

        def place_block(i, _, p=p, order=order):
            natural = 0
            for k, stage in enumerate(order):
                dim = natural_dim(stage, *sizes)
                natural = natural + lax.rem(i // (1 << (bits - 1 - k)), 2) * (1 << (bits - 1 - dim))
            wide = columns[p][1]
            all_ref[natural, :, pl.ds(*columns[p])] = gathered[p][i, :, :wide]
            if p == count - 1:
                mix_all_ref[natural] = gathered[p][i, :, wide:]
            return 0

        lax.fori_loop(0, 1 << bits, place_block, 0)
    for copy in copies:
        copy.wait_send()


def down_kernel(orders, columns, *refs):
    count = len(orders)
    lhs, refs = refs[: count // 2], refs[count // 2 :]
    w_ref, hid_ref, out_ref = refs[:3]
    bufs, gots = refs[3 : 3 + count], refs[3 + count : 3 + 2 * count]
    send_sem, recv_sem = refs[3 + 2 * count :]
    greet(orders[0])

    def finish(p, total):
        cols = pl.ds(*columns[p])
        out_ref[:, cols] = (hid_ref[:, cols] + total).astype(out_ref.dtype)

    reduce_scatter(orders, columns, lhs, w_ref, bufs, gots, send_sem, recv_sem, finish)


def experts_kernel(orders, columns, sizes, *refs):
    x_ref, mix_ref, gate_hbm, up_hbm, down_hbm, hid_ref, out_ref = refs[:7]
    count = len(orders)
    refs = refs[7:]
    bufs, gots, lhs = refs[:count], refs[count : 2 * count], refs[2 * count : 2 * count + count // 2]
    gate_ref, up_ref, down_ref, send_sem, recv_sem, load_sem = refs[2 * count + count // 2 :]
    experts, _, hidden_units = gate_ref.shape

    def load(e):
        return (
            pltpu.make_async_copy(gate_hbm.at[e], gate_ref.at[e], load_sem.at[0, e]),
            pltpu.make_async_copy(up_hbm.at[e], up_ref.at[e], load_sem.at[1, e]),
        )

    for e in range(experts):
        for copy in load(e):
            copy.start()
    load_down = pltpu.make_async_copy(down_hbm, down_ref, load_sem.at[2, 0])
    load_down.start()
    greet(orders[0])
    bits = len(orders[0])
    block = hid_ref.shape[0]

    def one_expert(e, _):
        for copy in load(e):
            copy.wait()
        gate = jnp.dot(x_ref[...], gate_ref[e], preferred_element_type=jnp.float32)
        up = jnp.dot(x_ref[...], up_ref[e], preferred_element_type=jnp.float32)
        active = (gate / (1.0 + jnp.exp(-gate)) * up * mix_ref[e]).astype(jnp.bfloat16)
        cols = pl.ds(pl.multiple_of(e * hidden_units, hidden_units), hidden_units)
        for order, rows_ref in zip(orders, lhs):
            dims = [natural_dim(stage, *sizes) for stage in order]
            for i in range(1 << bits):
                natural = sum((i >> (bits - 1 - k) & 1) << (bits - 1 - d) for k, d in enumerate(dims))
                rows_ref[pl.ds(i * block, block), cols] = active[natural * block : (natural + 1) * block]
        return 0

    lax.fori_loop(0, experts, one_expert, 0)
    load_down.wait()

    def finish(p, total):
        cols = pl.ds(*columns[p])
        out_ref[:, cols] = (hid_ref[:, cols] + total).astype(out_ref.dtype)

    reduce_scatter(orders, columns, lhs, down_ref, bufs, gots, send_sem, recv_sem, finish)


def call_experts(orders, columns, sizes, normed, mix, w_gate, w_up, w_down, own_hidden):
    vmem, anywhere = pl.BlockSpec(memory_space=pltpu.VMEM), pl.BlockSpec(memory_space=pl.ANY)
    block, model_width = own_hidden.shape
    rows = normed.shape[0]
    bufs = [pltpu.VMEM((rows // block, block, w), jnp.bfloat16) for _, w in columns]
    lhs = [pltpu.VMEM((rows, w_down.shape[0]), jnp.bfloat16)] * (len(orders) // 2)
    sems = [pltpu.SemaphoreType.DMA((len(columns), len(orders[0])))] * 2
    return pl.pallas_call(
        functools.partial(experts_kernel, orders, columns, sizes),
        out_shape=jax.ShapeDtypeStruct((block, model_width), jnp.bfloat16),
        in_specs=[vmem, vmem, anywhere, anywhere, anywhere, vmem],
        out_specs=vmem,
        scratch_shapes=bufs * 2
        + lhs
        + [pltpu.VMEM(w.shape, jnp.bfloat16) for w in (w_gate, w_up, w_down)]
        + sems
        + [pltpu.SemaphoreType.DMA((3, w_gate.shape[0]))],
        compiler_params=pltpu.CompilerParams(
            collective_id=2, has_side_effects=True, vmem_limit_bytes=VMEM_BYTES
        ),
        cost_estimate=pl.CostEstimate(
            flops=6 * rows * w_down.size, bytes_accessed=6 * w_down.size, transcendentals=0
        ),
    )(normed, mix.T[:, :, None], w_gate, w_up, w_down, own_hidden)


def call(kernel, collective_id, args, outs, blocks, block, columns, extra, steps, cost):
    vmem = pl.BlockSpec(memory_space=pltpu.VMEM)
    bufs = [pltpu.VMEM((blocks, block, w), jnp.bfloat16) for _, w in columns]
    sems = [pltpu.SemaphoreType.DMA((len(columns), steps))] * (4 if extra else 2)
    wider = [w for _, w in columns[:-1]] + [columns[-1][1] + extra]
    gathered = [pltpu.VMEM((blocks, block, w), jnp.bfloat16) for w in wider] if extra else []
    return pl.pallas_call(
        kernel,
        out_shape=outs,
        in_specs=[vmem] * len(args),
        out_specs=jax.tree.map(lambda _: vmem, outs),
        scratch_shapes=bufs * 2 + gathered + sems,
        compiler_params=pltpu.CompilerParams(
            collective_id=collective_id, has_side_effects=True, vmem_limit_bytes=VMEM_BYTES
        ),
        cost_estimate=cost,
    )(*args)


def attend(queries, latent_cache, new_latents):
    tok_rows = queries.shape[0]
    context = latent_cache.shape[0]
    key_rows = jnp.concatenate([latent_cache, new_latents], axis=0)
    scores = jnp.einsum("thc,kc->htk", queries, key_rows, preferred_element_type=jnp.float32) * (
        VDIM + ROPE
    ) ** (-0.5)
    query_pos = jnp.arange(tok_rows, dtype=jnp.int32)[:, None]
    key_pos = jnp.arange(key_rows.shape[0], dtype=jnp.int32)[None, :] - context
    scores = jnp.where((key_pos <= query_pos)[None], scores, -jnp.inf)
    row_peak = jnp.max(scores, axis=2, keepdims=True)
    exp_scores = jnp.exp(scores - row_peak)
    attn_probs = (exp_scores / jnp.sum(exp_scores, axis=2, keepdims=True)).astype(jnp.bfloat16)
    return jnp.einsum(
        "htk,kl->htl", attn_probs, key_rows[:, :LATENT], preferred_element_type=jnp.float32
    ).astype(jnp.bfloat16)


def per_device(
    queries,
    latent_cache,
    new_latents,
    residual,
    w_uv,
    w_out,
    norm_gain,
    expert_ids,
    gate_weights,
    w_gate,
    w_up,
    w_down,
):
    group_count = lax.axis_size("expert")
    tok_rows = queries.shape[0]
    head_count = queries.shape[1]
    local_experts = w_gate.shape[0]
    experts_all = local_experts * group_count

    block = residual.shape[0]
    first = lax.axis_index("tensor") * block
    own_ids = lax.dynamic_slice_in_dim(expert_ids, first, block, 0)
    own_weights = lax.dynamic_slice_in_dim(gate_weights, first, block, 0)
    chosen = own_ids[:, :, None] == jnp.arange(experts_all, dtype=jnp.int32)
    mix = jnp.sum(jnp.where(chosen, own_weights[:, :, None], 0.0), axis=1)
    high = lax.reduce_precision(mix, 8, 7)
    extra = -(-2 * experts_all // 128) * 128
    parts = jnp.concatenate([high, mix - high], axis=1).astype(jnp.bfloat16)
    parts = jnp.pad(parts, ((0, 0), (0, extra - 2 * experts_all)))

    attended = attend(queries, latent_cache, new_latents)
    if w_uv.shape[0] % LATENT == 0:
        attended = lax.all_to_all(attended, "expert", split_axis=0, concat_axis=0, tiled=True)
        own_heads = w_uv.shape[0] // LATENT
        columns = jnp.einsum(
            "ghtl,hlv->gthv",
            attended.reshape(group_count, own_heads, tok_rows, LATENT),
            w_uv.reshape(own_heads, LATENT, VDIM),
            preferred_element_type=jnp.float32,
        ).astype(jnp.bfloat16)
    else:
        uv_rows = lax.all_gather(w_uv, "expert", axis=0, tiled=True)
        head_values = jnp.einsum(
            "htl,hlv->thv",
            attended,
            uv_rows.reshape(head_count, LATENT, VDIM),
            preferred_element_type=jnp.float32,
        ).astype(jnp.bfloat16)
        columns = head_values.reshape(tok_rows, group_count, -1)
        columns = lax.all_to_all(columns, "expert", split_axis=1, concat_axis=0, tiled=True)
    columns = columns.reshape(group_count * tok_rows, -1)
    tensor_n = lax.axis_size("tensor")
    sizes = (group_count, tensor_n)
    orders = stage_orders(*sizes)
    model_width = residual.shape[1]
    cut = piece_columns(model_width, len(orders))
    blocks = group_count * tensor_n
    steps = len(orders[0])
    flops = 2 * blocks * block * w_out.size
    own_hidden, normed, mix_all = call(
        functools.partial(attention_out_kernel, orders, cut, sizes),
        0,
        [in_order(columns, o, *sizes) for o in orders[: len(orders) // 2]]
        + [w_out, residual, norm_gain.reshape(1, model_width), parts],
        (
            jax.ShapeDtypeStruct((block, model_width), jnp.float32),
            jax.ShapeDtypeStruct((blocks, block, model_width), jnp.bfloat16),
            jax.ShapeDtypeStruct((blocks, block, extra), jnp.bfloat16),
        ),
        blocks,
        block,
        cut,
        extra,
        steps,
        pl.CostEstimate(flops=flops, bytes_accessed=w_out.size * 2, transcendentals=0),
    )
    normed = normed.reshape(blocks * block, model_width)
    mix_all = mix_all.reshape(blocks * block, extra).astype(jnp.float32)
    mix_all = mix_all[:, :experts_all] + mix_all[:, experts_all : 2 * experts_all]
    mine = lax.axis_index("expert") * local_experts
    mix = lax.dynamic_slice_in_dim(mix_all, mine, local_experts, 1)

    held_bytes = 2 * (3 * w_down.size + 3 * normed.size + 3 * normed.shape[0] * w_down.size // model_width)
    if held_bytes < VMEM_BYTES * 3 // 4:
        down_rows = w_down.reshape(-1, model_width)
        return call_experts(orders, cut, sizes, normed, mix, w_gate, w_up, down_rows, own_hidden)

    gate_part = jnp.einsum("nd,edf->nef", normed, w_gate, preferred_element_type=jnp.float32)
    up_part = jnp.einsum("nd,edf->nef", normed, w_up, preferred_element_type=jnp.float32)
    active = (jax.nn.silu(gate_part) * up_part * mix[:, :, None]).astype(jnp.bfloat16)
    active = active.reshape(blocks * block, -1)
    return call(
        functools.partial(down_kernel, orders, cut),
        1,
        [in_order(active, o, *sizes) for o in orders[: len(orders) // 2]] + [w_down.reshape(-1, model_width), own_hidden],
        jax.ShapeDtypeStruct((block, model_width), jnp.bfloat16),
        blocks,
        block,
        cut,
        0,
        steps,
        pl.CostEstimate(flops=2 * blocks * block * w_down.size, bytes_accessed=w_down.size * 2, transcendentals=0),
    )


def solution(mesh):
    placed = (
        P("expert", "tensor", None),
        P("expert", None),
        P("expert", None),
        P(("expert", "tensor"), None),
        P(("tensor", "expert"), None),
        P(("tensor", "expert"), None),
        P(),
        P("expert", None),
        P("expert", None),
        P("expert", None, "tensor"),
        P("expert", None, "tensor"),
        P("expert", "tensor", None),
    )
    return jax.shard_map(
        per_device,
        mesh=mesh,
        in_specs=placed,
        out_specs=P(("expert", "tensor"), None),
        check_vma=False,
    )
```
